256 devices in a mesh: ri: 32 (over z, y), ao: 8 (over x, core).
Axes of the slice: x: 4, y: 4, z: 8, core: 2. Of those that a mesh axis runs over, the one named last changes fastest.
Arguments:
- three_center: bfloat16 [1024, 512, 512], P('ao', 'ri'), may hold values from -0.0234375 to 0.0234375
- tile_mask: int32 [16, 16, 16], replicated, may hold values 0 or 1
- atom_order: int32 [16], replicated, may hold values from 0 to 15, each once
- green_occ: bfloat16 [512, 512], P('ao')
- green_virt: bfloat16 [512, 512], P('ao')
Outputs:
- response: float32 [1024, 1024], P('ri', 'ao')
The draws below stay inside these ranges and needn't reach their ends.
Inputs may be any that keep to these rules, and one draw needn't show every extreme that they name: `atom_order`: each atom appears once. `tile_mask`: 1 keeps a tile, 0 screens it out.
All inputs are finite; a program needn't handle non-finite values.
Results may differ from the reference program's by a relative error of at most 0.0004.
Values may be sent and summed in bfloat16 or wider, within the bound.
No kernel may reach another device: no remote copies, remote signals or barrier semaphores. Data moves between devices by JAX's collectives and lax.ppermute only.
A program may use at most 64 MiB of HBM per device.

```python
import jax
import jax.numpy as jnp
from jax import lax

AO_ATOM = 32
RI_ATOM = 64
NRI = 1024
ATOMS = 16
NAO = 512


def green_matrix(key, spread):
    diag_key, off_key = jax.random.split(key, 2)
    diagonal = jax.random.uniform(diag_key, (NAO,), jnp.float32, 0.5, 1.5)
    offdiag = jax.random.normal(off_key, (NAO, NAO), jnp.float32) * (spread / NAO ** 0.5)
    rows = lax_iota(NAO)[:, None]
    cols = lax_iota(NAO)[None, :]
    eye = (rows == cols).astype(jnp.float32)
    return (offdiag + eye * diagonal[None, :]).astype(jnp.bfloat16)


def lax_iota(count):
    return jnp.arange(count, dtype=jnp.int32)


def draw_green_occ(key, part):
    key = jax.random.fold_in(key, 11)
    return green_matrix(key, 0.6)


def draw_green_virt(key, part):
    key = jax.random.fold_in(key, 23)
    return green_matrix(key, 0.5)


def plant(array, stream_key, smallest, high):
    longest = array.shape.index(max(array.shape))
    spots = []
    for shift in (0, 1):
        where = [jax.random.randint(jax.random.fold_in(stream_key, axis), (), 0, length) for axis, length in enumerate(array.shape)]
        where[longest] = (where[longest] + shift) % array.shape[longest]
        spots.append(tuple(where))
    return array.at[spots[0]].set(smallest).at[spots[1]].set(high)


def levels(rng, extent, shards, low, largest):
    def one(axis_at, shards_of):
        draws = jax.random.uniform(jax.random.fold_in(jax.random.fold_in(rng, 6), axis_at), (shards_of,), jnp.float32, low / len(shards), largest / len(shards))
        return jnp.repeat(jnp.exp(draws), extent[axis_at] // shards_of).reshape((-1,) + (1,) * (len(extent) - axis_at - 1))

    level = one(*shards[0])
    for cut in shards[1:]:
        level = level * one(*cut)
    return level


def centred(rng, extent, scale, bound, cuts=(), kind=jnp.bfloat16):
    result = jax.random.normal(rng, extent, jnp.float32) * scale
    if len(cuts) > 0:
        result = levels(rng, extent, cuts, -0.22, 0.18) * result
    return jnp.clip(result, min=-bound, max=bound).astype(kind)


def setup_inputs(seed: int = 0) -> dict:
    key_of = jax.random.split(jax.random.key(seed), 6)
    return {
        "three_center": centred(key_of[0], (NRI, NAO, NAO), (2.0 / NAO), 0.0234375, ((0, 8), (1, 32))),
        "tile_mask": plant((jax.random.randint(key_of[1], (ATOMS, ATOMS, ATOMS), 0, 4) < 3).astype(jnp.int32), jax.random.fold_in(key_of[1], 1), 0, 1),
        "atom_order": jax.random.permutation(key_of[2], ATOMS).astype(jnp.int32),
        "green_occ": draw_green_occ(jax.random.fold_in(key_of[5], 71), 0),
        "green_virt": draw_green_virt(jax.random.fold_in(key_of[5], 71), 0),
    }


def reference(three_center, tile_mask, atom_order, green_occ, green_virt):
    slots = (atom_order[:, None] * AO_ATOM + jnp.arange(AO_ATOM, dtype=jnp.int32)[None, :]).reshape(-1).astype(jnp.int32)
    natural = jnp.zeros_like(three_center).at[:, slots, :].set(three_center)

    def per_function(index):
        raw_tile = natural[index]
        mask_row = tile_mask[index // RI_ATOM]
        expanded = jnp.repeat(jnp.repeat(mask_row, AO_ATOM, axis=0), AO_ATOM, axis=1)
        screened = raw_tile * expanded.astype(jnp.bfloat16)
        half = jnp.dot(screened, green_virt, preferred_element_type=jnp.float32).astype(jnp.bfloat16)
        dressed = jnp.dot(green_occ.T, half, preferred_element_type=jnp.float32).astype(jnp.bfloat16)
        return screened, dressed

    screened_all, dressed_all = lax.map(per_function, jnp.arange(NRI, dtype=jnp.int32))
    flat_dressed = dressed_all.reshape(NRI, NAO * NAO)
    flat_screened = screened_all.reshape(NRI, NAO * NAO)
    return lax.dot_general(flat_dressed, flat_screened, (((1,), (1,)), ((), ())), preferred_element_type=jnp.float32)
```

```python
import jax
import jax.numpy as jnp
from jax import lax
from jax.experimental import pallas as pl
from jax.experimental.pallas import tpu as pltpu
from jax.sharding import PartitionSpec as P

AO_ATOM = 32
RI_ATOM = 64
VMEM_LIMIT = 40 * 1024 * 1024
NT = (((1,), (1,)), ((), ()))


def dot(left, right, dims=(((1,), (0,)), ((), ()))):
    return lax.dot_general(left, right, dims, preferred_element_type=jnp.float32)


def swap_matrix(outer, inner):
    size = outer * inner
    row = lax.broadcasted_iota(jnp.int32, (size, size), 0)
    col = lax.broadcasted_iota(jnp.int32, (size, size), 1)
    source = (row % outer) * inner + row // outer
    return (col == source).astype(jnp.bfloat16)


def transpose_rows(block):
    width = block.shape[1]
    row = lax.broadcasted_iota(jnp.int32, (width, width), 0)
    col = lax.broadcasted_iota(jnp.int32, (width, width), 1)
    return dot((row == col).astype(jnp.bfloat16), block, NT).astype(jnp.bfloat16)


def send_columns(columns, out_ref, first):
    ri_count, _, sig_count, p_count = out_ref.shape
    for at in range(2):
        part = columns[:, at * p_count : (at + 1) * p_count]
        out_ref[:, first + at, :, :] = part.reshape(ri_count, sig_count, p_count)


def screen_kernel(mask_ref, order_ref, tensor_ref, rows_ref, send_ref):
    p_count, row_count, width = tensor_ref.shape
    group = 16
    atom = order_ref[(lax.axis_index("ri") * row_count) // AO_ATOM]
    first_ri_atom = (lax.axis_index("ao") * p_count) // RI_ATOM
    lane_atom = lax.broadcasted_iota(jnp.int32, (1, width), 1) // AO_ATOM
    masks = []
    for ri_atom in range(p_count // RI_ATOM):
        mask = jnp.zeros((1, width), jnp.float32)
        for at in range(width // AO_ATOM):
            tile = mask_ref[first_ri_atom + ri_atom, atom, at].astype(jnp.float32)
            mask = jnp.where(lane_atom == at, tile, mask)
        masks.append(mask)
    swap = swap_matrix(group, row_count)
    for block in range(p_count // group):
        span = pl.ds(block * group, group)
        stored = tensor_ref[span].reshape(group * row_count, width)
        by_rows = dot(swap, stored) * masks[block * group // RI_ATOM]
        rows_ref[:, span, :] = by_rows.astype(jnp.bfloat16).reshape(row_count, group, width)
    for row in range(0, send_ref.shape[1], 2):
        pair = rows_ref[row : row + 2].reshape(2 * p_count, width)
        send_columns(transpose_rows(pair), send_ref, row)


def transpose_kernel(first_row, rows_ref, send_ref):
    _, p_count, width = rows_ref.shape
    for row in range(0, send_ref.shape[1], 2):
        at = first_row + row
        pair = rows_ref[at : at + 2].reshape(2 * p_count, width)
        send_columns(transpose_rows(pair), send_ref, row)


def half_kernel(order_ref, rows_ref, greens_ref, send_ref, occ_ref):
    row_count, p_count, width = rows_ref.shape
    local = greens_ref.shape[1] // 2
    occ = greens_ref[:, :local, :].reshape(width, width)
    virt = greens_ref[:, local:, :].reshape(width, width)
    virt_t = transpose_rows(virt)
    for row in range(0, row_count, 2):
        pair = rows_ref[row : row + 2].reshape(2 * p_count, width)
        send_columns(dot(virt_t, pair, NT).astype(jnp.bfloat16), send_ref, row)
    lane = lax.broadcasted_iota(jnp.int32, (AO_ATOM, width), 1)
    inner = lax.broadcasted_iota(jnp.int32, (AO_ATOM, width), 0)
    picks = [
        (lane == inner + order_ref[slot] * AO_ATOM).astype(jnp.bfloat16)
        for slot in range(width // AO_ATOM)
    ]
    pick = jnp.concatenate(picks, axis=0)
    by_nu = dot(pick, occ, NT).astype(jnp.bfloat16)
    occ_ref[...] = dot(by_nu, pick, NT).astype(jnp.bfloat16)


def dress_kernel(half_ref, occ_ref, dressed_ref, by_sig):
    ri_count, row_count, sig_count, p_count = half_ref.shape
    swap = swap_matrix(row_count, sig_count)
    unswap = swap_matrix(sig_count, row_count)
    block_rows = row_count * sig_count
    for r in range(0, ri_count, 2):
        pair = [half_ref[r + at].reshape(block_rows, p_count) for at in range(2)]
        swapped = dot(swap, jnp.concatenate(pair, axis=1)).astype(jnp.bfloat16)
        for at in range(2):
            part = swapped[:, at * p_count : (at + 1) * p_count]
            by_sig[:, pl.ds((r + at) * row_count, row_count), :] = part.reshape(
                sig_count, row_count, p_count
            )
    occ_t = occ_ref[...]
    for sig in range(0, sig_count, 2):
        pair = jnp.concatenate([by_sig[sig], by_sig[sig + 1]], axis=1)
        dressed = dot(occ_t, pair).astype(jnp.bfloat16)
        by_sig[sig] = dressed[:, :p_count]
        by_sig[sig + 1] = dressed[:, p_count:]
    for r in range(ri_count):
        block = by_sig[:, pl.ds(r * row_count, row_count), :].reshape(block_rows, p_count)
        turned = lax.dot_general(
            block, unswap, (((0,), (1,)), ((), ())), preferred_element_type=jnp.float32
        )
        dressed_ref[r] = turned.astype(jnp.bfloat16)


def product_kernel(has_init, *refs):
    if has_init:
        dressed_ref, gathered_ref, init_ref, out_ref = refs
    else:
        dressed_ref, gathered_ref, out_ref = refs
    ao_count, blocks, depth, p_count = gathered_ref.shape
    piece = out_ref.shape[1]
    pieces = p_count // piece

    @pl.when(pl.program_id(0) == 0)
    def _():
        if has_init:
            out_ref[...] = init_ref[...]
        else:
            out_ref[...] = jnp.zeros_like(out_ref)

    left = jnp.concatenate([dressed_ref[r] for r in range(blocks)], axis=1)
    for at in range(0, ao_count, 2):
        pair = [gathered_ref[at + k].reshape(blocks * depth, p_count) for k in range(2)]
        part = dot(left, jnp.concatenate(pair, axis=1))
        for k in range(2):
            for j in range(pieces):
                out_ref[(at + k) * pieces + j] += part[
                    j * piece : (j + 1) * piece, k * p_count : (k + 1) * p_count
                ]


def params():
    return pltpu.CompilerParams(vmem_limit_bytes=VMEM_LIMIT)


VMEM = pl.BlockSpec(memory_space=pltpu.VMEM)
SMEM = pl.BlockSpec(memory_space=pltpu.SMEM)


def product(dressed, gathered, column, piece, init=None):
    ri_count, p_count, _ = dressed.shape
    ao_count, _, rows, sig_count, _ = gathered.shape
    depth = rows * sig_count
    gathered = gathered.reshape(ao_count, ri_count, depth, p_count)
    blocks = 4
    out_shape = (ao_count * p_count // piece, piece, p_count)
    in_specs = [
        pl.BlockSpec((blocks, p_count, depth), lambda k: (k, 0, column)),
        pl.BlockSpec((ao_count, blocks, depth, p_count), lambda k: (0, k, 0, 0)),
    ]
    operands = [dressed, gathered]
    if init is not None:
        in_specs.append(pl.BlockSpec(out_shape, lambda k: (0, 0, 0)))
        operands.append(init)
    return pl.pallas_call(
        lambda *refs: product_kernel(init is not None, *refs),
        grid=(ri_count // blocks,),
        in_specs=in_specs,
        out_specs=pl.BlockSpec(out_shape, lambda k: (0, 0, 0)),
        out_shape=jax.ShapeDtypeStruct(out_shape, jnp.float32),
        compiler_params=params(),
        cost_estimate=pl.CostEstimate(
            flops=2 * p_count * gathered.size, bytes_accessed=2 * gathered.size, transcendentals=0
        ),
    )(*operands)


def shards(three_center, tile_mask, atom_order, green_occ, green_virt):
    p_count, row_count, width = three_center.shape
    ri_count, ao_count = lax.axis_size("ri"), lax.axis_size("ao")
    sig_count = width // ri_count
    first_rows = row_count // 2

    def send_shape(rows):
        return jax.ShapeDtypeStruct((ri_count, rows, sig_count, p_count), jnp.bfloat16)

    def spread(block):
        return lax.all_to_all(block, "ri", split_axis=0, concat_axis=0, tiled=True)

    greens = lax.all_gather(jnp.concatenate([green_occ, green_virt], axis=0), "ao", axis=0)

    rows, send_first = pl.pallas_call(
        screen_kernel,
        in_specs=[SMEM, SMEM, VMEM],
        out_specs=[VMEM, VMEM],
        out_shape=[
            jax.ShapeDtypeStruct((row_count, p_count, width), jnp.bfloat16),
            send_shape(first_rows),
        ],
        compiler_params=params(),
    )(tile_mask, atom_order, three_center)
    first = spread(send_first)

    send_second = pl.pallas_call(
        lambda *refs: transpose_kernel(first_rows, *refs),
        in_specs=[VMEM],
        out_specs=VMEM,
        out_shape=send_shape(row_count - first_rows),
        compiler_params=params(),
        cost_estimate=pl.CostEstimate(
            flops=rows.size * width, bytes_accessed=4 * rows.size, transcendentals=0
        ),
    )(rows)
    second = spread(send_second)

    send_half, occ_slots = pl.pallas_call(
        half_kernel,
        in_specs=[SMEM, VMEM, VMEM],
        out_specs=[VMEM, VMEM],
        out_shape=[send_shape(row_count), jax.ShapeDtypeStruct((width, width), jnp.bfloat16)],
        compiler_params=params(),
        cost_estimate=pl.CostEstimate(
            flops=2 * rows.size * width, bytes_accessed=6 * rows.size, transcendentals=0
        ),
    )(atom_order, rows, greens)
    first_all = lax.all_gather(first, "ao", axis=0)
    second_all = lax.all_gather(second, "ao", axis=0)
    half = spread(send_half)

    dressed = pl.pallas_call(
        dress_kernel,
        in_specs=[VMEM, VMEM],
        out_specs=VMEM,
        out_shape=jax.ShapeDtypeStruct((ri_count, p_count, row_count * sig_count), jnp.bfloat16),
        scratch_shapes=[pltpu.VMEM((sig_count, width, p_count), jnp.bfloat16)],
        compiler_params=params(),
        cost_estimate=pl.CostEstimate(
            flops=2 * rows.size * width, bytes_accessed=6 * rows.size, transcendentals=0
        ),
    )(half, occ_slots)

    piece = ao_count * p_count // ri_count
    partial = product(dressed, first_all, 0, piece)
    partial = product(dressed, second_all, 1, piece, partial)
    summed = spread(partial).sum(axis=0)
    pieces = p_count // piece
    moves = []
    for column in range(ao_count):
        for j in range(pieces):
            for row_block in range(ao_count):
                source = (column * pieces + j) * ao_count + row_block
                target = (row_block * pieces + j) * ao_count + column
                moves.append((source, target))
    return lax.ppermute(summed, ("ri", "ao"), moves)


def solution(mesh):
    placed = (P("ao", "ri", None), P(), P(), P("ao", None), P("ao", None))
    return jax.shard_map(
        shards, mesh=mesh, in_specs=placed, out_specs=P("ri", "ao"), check_vma=False
    )
```

```python
import jax
import jax.numpy as jnp
from jax import lax
from jax.experimental import pallas as pl
from jax.experimental.pallas import tpu as pltpu
from jax.sharding import PartitionSpec as P

AO_ATOM = 32
RI_ATOM = 64
X_SIZE = 4
CORES = 2
SHIFTS = (0, 1, X_SIZE - 1, 2)
FIRST_ROWS = 6
VMEM_LIMIT = 24 * 1024 * 1024
NT = (((1,), (1,)), ((), ()))
TN = (((0,), (0,)), ((), ()))
VMEM = pl.BlockSpec(memory_space=pltpu.VMEM)
HBM = pl.BlockSpec(memory_space=pltpu.HBM)


def position():
    index = lax.axis_index("ao")
    return index // CORES, index % CORES


def dot(left, right, dims=(((1,), (0,)), ((), ()))):
    return lax.dot_general(left, right, dims, preferred_element_type=jnp.float32)


def swap_matrix(outer, inner):
    size = outer * inner
    row = lax.broadcasted_iota(jnp.int32, (size, size), 0)
    col = lax.broadcasted_iota(jnp.int32, (size, size), 1)
    source = (row % outer) * inner + row // outer
    return (col == source).astype(jnp.bfloat16)


def screened_rows(refs, rows, first_row):
    order_hbm, mask_hbm, tensor_hbm, order_ref, mask_ref, tensor_ref, sems = refs
    p_count, stored_rows, width = tensor_ref.shape
    row_count = rows.shape[0]
    atoms = mask_ref.shape[2]
    group = 16
    copies = [
        pltpu.make_async_copy(order_hbm, order_ref, sems.at[0]),
        pltpu.make_async_copy(mask_hbm, mask_ref, sems.at[1]),
    ]
    for block in range(p_count // group):
        span = pl.ds(block * group, group)
        copies.append(
            pltpu.make_async_copy(tensor_hbm.at[span], tensor_ref.at[span], sems.at[2 + block])
        )
    for copy in copies:
        copy.start()
    lane = lax.broadcasted_iota(jnp.int32, (atoms, width), 1)
    spread = (lane // AO_ATOM == lax.broadcasted_iota(jnp.int32, (atoms, width), 0)).astype(
        jnp.bfloat16
    )
    first_ri_atom = (lax.axis_index("ao") * p_count) // RI_ATOM
    copies[0].wait()
    copies[1].wait()
    atom = order_ref[(lax.axis_index("ri") * stored_rows) // AO_ATOM]
    masks = []
    for ri_atom in range(p_count // RI_ATOM):
        tiles = mask_ref[first_ri_atom + ri_atom, pl.ds(atom, 1), :].astype(jnp.float32)
        tiles = jnp.broadcast_to(tiles.astype(jnp.bfloat16), (8, atoms))
        masks.append(dot(tiles, spread)[:1].astype(jnp.bfloat16))
    for block in range(p_count // group):
        copies[2 + block].wait()
        span = pl.ds(block * group, group)
        by_rows = jnp.swapaxes(tensor_ref[span], 0, 1)[first_row : first_row + row_count]
        rows[:, span, :] = by_rows * masks[block * group // RI_ATOM][None]


def send_rows(rows, send_ref, turn):
    ri_count, row_count, sig_count, p_count = send_ref.shape
    width = rows.shape[2]
    for row in range(0, row_count, 2):
        columns = turn(rows[row : row + 2].reshape(2 * p_count, width))
        for at in range(2):
            part = columns[:, at * p_count : (at + 1) * p_count]
            send_ref[:, row + at, :, :] = part.reshape(ri_count, sig_count, p_count)


def screen_kernel(first_row, *refs):
    inputs, (send_ref, rows), scratch = refs[:3], refs[3:5], refs[5:]
    screened_rows(inputs + scratch, rows, first_row)
    send_rows(rows, send_ref, lambda pair: pair.T)


def half_kernel(*refs):
    inputs, pair_refs, refs = refs[:3], refs[3 : 3 + X_SIZE], refs[3 + X_SIZE :]
    (send_ref, occ_ref, rows, greens), scratch = refs[:4], refs[4:]
    screened_rows(inputs + scratch, rows, 0)
    width = rows.shape[2]
    x, core = position()
    for pair_ref, shift in zip(pair_refs, SHIFTS):
        for at in range(CORES):
            source = (x + X_SIZE - shift) % X_SIZE * CORES + (core if at == 0 else 1 - core)
            greens[source] = pair_ref[at]
    local = greens.shape[1] // 2
    occ = greens[:, :local, :].reshape(width, width)
    virt_t = greens[:, local:, :].reshape(width, width).T
    send_rows(rows, send_ref, lambda pair: dot(virt_t, pair, NT).astype(jnp.bfloat16))
    order_ref = scratch[0]
    lane = lax.broadcasted_iota(jnp.int32, (AO_ATOM, width), 1)
    inner = lax.broadcasted_iota(jnp.int32, (AO_ATOM, width), 0)
    picks = [
        (lane == inner + order_ref[slot] * AO_ATOM).astype(jnp.bfloat16)
        for slot in range(width // AO_ATOM)
    ]
    pick = jnp.concatenate(picks, axis=0)
    by_nu = dot(pick, occ, NT).astype(jnp.bfloat16)
    occ_ref[...] = dot(by_nu, pick, NT).astype(jnp.bfloat16)


def dress_kernel(half_ref, occ_hbm, first_ref, second_ref, by_sig, occ_ref, sem):
    ri_count, row_count, sig_count, p_count = half_ref.shape
    copy = pltpu.make_async_copy(occ_hbm, occ_ref, sem)
    copy.start()
    swap = swap_matrix(row_count, sig_count)
    unswap = swap_matrix(sig_count, row_count)
    block_rows = row_count * sig_count
    first_rows = first_ref.shape[1]

    def rows_of(r):
        return pl.ds(pl.multiple_of(r * row_count, row_count), row_count)

    def to_sig(i, carry):
        pair = [half_ref[2 * i + at].reshape(block_rows, p_count) for at in range(2)]
        swapped = dot(swap, jnp.concatenate(pair, axis=1)).astype(jnp.bfloat16)
        for at in range(2):
            part = swapped[:, at * p_count : (at + 1) * p_count]
            by_sig[:, rows_of(2 * i + at), :] = part.reshape(sig_count, row_count, p_count)
        return carry

    def dress(i, carry):
        pair = jnp.concatenate([by_sig[2 * i], by_sig[2 * i + 1]], axis=1)
        dressed = dot(occ_ref[...], pair).astype(jnp.bfloat16)
        by_sig[2 * i] = dressed[:, :p_count]
        by_sig[2 * i + 1] = dressed[:, p_count:]
        return carry

    def to_rows(i, carry):
        pair = [
            by_sig[:, rows_of(2 * i + at), :].reshape(block_rows, p_count) for at in range(2)
        ]
        swapped = dot(unswap, jnp.concatenate(pair, axis=1)).astype(jnp.bfloat16)
        for at in range(2):
            part = swapped[:, at * p_count : (at + 1) * p_count]
            first_ref[2 * i + at] = part[:first_rows]
            second_ref[2 * i + at] = part[first_rows:]
        return carry

    lax.fori_loop(0, ri_count // 2, to_sig, 0, unroll=True)
    copy.wait()
    lax.fori_loop(0, sig_count // 2, dress, 0, unroll=True)
    lax.fori_loop(0, ri_count // 2, to_rows, 0, unroll=True)


def product_kernel(has_init, own_ref, other_ref, *refs):
    ri_count, depth, p_count = own_ref.shape
    out_ref, total = refs[-2:]
    init_ref, chunk = (refs[-3], refs[:-3]) if has_init else (None, refs[:-2])
    blocks = 8
    for first in range(0, ri_count, blocks):
        sources = [(ref, first) for ref in (own_ref, other_ref) + chunk[: X_SIZE - 1]]
        far = chunk[X_SIZE - 1 :]
        half, inner = divmod(first, ri_count // len(far))
        sources.append((far[half], inner))
        parts = [ref[at : at + blocks].reshape(blocks * depth, p_count) for ref, at in sources]
        part = dot(
            jnp.concatenate(parts[:CORES], axis=1), jnp.concatenate(parts[CORES:], axis=1), TN
        )
        if first == 0:
            total[...] = part + init_ref[...] if has_init else part
        else:
            total[...] += part
    if not has_init:
        out_ref[...] = total[...]
        return
    x, core = position()
    pieces = out_ref.shape[1]
    for at in range(CORES):
        holder = core if at == 0 else 1 - core
        for k in range(X_SIZE):
            column = (x + X_SIZE - SHIFTS[k]) % X_SIZE
            part = total[at * p_count : (at + 1) * p_count, k * p_count : (k + 1) * p_count]
            out_ref[holder * X_SIZE + column] = part.reshape(pieces, p_count // pieces, p_count)


def in_hbm(array):
    return pltpu.with_memory_space_constraint(array, pltpu.HBM)


def params():
    return pltpu.CompilerParams(vmem_limit_bytes=VMEM_LIMIT)


def cost(flops, touched):
    return pl.CostEstimate(flops=flops, bytes_accessed=touched, transcendentals=0)


def product(own, other, gathered, pieces, init=None):
    ri_count, depth, p_count = own.shape
    sums = (CORES * p_count, X_SIZE * p_count)
    if init is None:
        out_shape = sums
    else:
        out_shape = (CORES * X_SIZE, pieces, p_count // pieces, p_count)
    operands = [own, other] + [block.reshape(-1, depth, p_count) for block in gathered]
    if init is not None:
        operands.append(init)
    return pl.pallas_call(
        lambda *refs: product_kernel(init is not None, *refs),
        in_specs=[VMEM] * len(operands),
        out_specs=VMEM,
        out_shape=jax.ShapeDtypeStruct(out_shape, jnp.float32),
        scratch_shapes=[pltpu.VMEM(sums, jnp.float32)],
        compiler_params=params(),
        cost_estimate=cost(2 * sums[0] * sums[1] * ri_count * depth, 12 * own.size),
    )(*operands)


def shards(three_center, tile_mask, atom_order, green_occ, green_virt):
    p_count, row_count, width = three_center.shape
    ri_count, ao_count = lax.axis_size("ri"), lax.axis_size("ao")
    sig_count = width // ri_count

    def send_shape(rows):
        return jax.ShapeDtypeStruct((ri_count, rows, sig_count, p_count), jnp.bfloat16)

    def spread(block):
        return lax.all_to_all(block, "ri", split_axis=0, concat_axis=0, tiled=True)

    def to_other_core(block):
        return lax.ppermute(block, "ao", [(i, i ^ 1) for i in range(ao_count)])

    def along_x(block, shift):
        moves = [(i, (i + CORES * shift) % ao_count) for i in range(ao_count)]
        return lax.ppermute(block, "ao", moves)

    def from_all_x(block):
        return [block] + [along_x(block, shift) for shift in SHIFTS[1:]]

    def from_all_x_in_two(block):
        half = ri_count // 2
        after, before = along_x(block, 1), along_x(block, -1)
        return [block, after, before, along_x(after[:half], 1), along_x(before[half:], -1)]

    tensor = [in_hbm(array) for array in (atom_order, tile_mask, three_center)]
    tensor_scratch = [
        pltpu.SMEM(atom_order.shape, jnp.int32),
        pltpu.VMEM(tile_mask.shape, jnp.int32),
        pltpu.VMEM(three_center.shape, jnp.bfloat16),
        pltpu.SemaphoreType.DMA((2 + p_count // 16,)),
    ]

    def rows_scratch(rows):
        return pltpu.VMEM((rows, p_count, width), jnp.bfloat16)

    def screen(first_row, rows):
        return pl.pallas_call(
            lambda *refs: screen_kernel(first_row, *refs),
            in_specs=[HBM] * 3,
            out_specs=VMEM,
            out_shape=send_shape(rows),
            scratch_shapes=[rows_scratch(rows)] + tensor_scratch,
            compiler_params=params(),
            cost_estimate=cost(0, 4 * three_center.size),
        )(*tensor)

    first = spread(screen(0, FIRST_ROWS))

    greens = jnp.concatenate([green_occ, green_virt], axis=0)
    greens = from_all_x(jnp.stack([greens, to_other_core(greens)]))

    send_second = screen(FIRST_ROWS, row_count - FIRST_ROWS)
    first, send_second, *greens = lax.optimization_barrier((first, send_second, *greens))
    first_all = from_all_x_in_two(first)
    second = spread(send_second)

    send_half, occ_slots = pl.pallas_call(
        half_kernel,
        in_specs=[HBM] * 3 + [VMEM] * X_SIZE,
        out_specs=[VMEM, VMEM],
        out_shape=[send_shape(row_count), jax.ShapeDtypeStruct((width, width), jnp.bfloat16)],
        scratch_shapes=[
            rows_scratch(row_count),
            pltpu.VMEM((ao_count, *greens[0].shape[1:]), jnp.bfloat16),
        ]
        + tensor_scratch,
        compiler_params=params(),
        cost_estimate=cost(2 * three_center.size * width, 6 * three_center.size),
    )(*tensor, *greens)
    second, send_half, *first_all = lax.optimization_barrier((second, send_half, *first_all))
    second_all = from_all_x(second)
    half = spread(send_half)

    def dressed_shape(rows):
        return jax.ShapeDtypeStruct((ri_count, rows * sig_count, p_count), jnp.bfloat16)

    dressed_first, dressed_second = pl.pallas_call(
        dress_kernel,
        in_specs=[VMEM, HBM],
        out_specs=[VMEM, VMEM],
        out_shape=[dressed_shape(FIRST_ROWS), dressed_shape(row_count - FIRST_ROWS)],
        scratch_shapes=[
            pltpu.VMEM((sig_count, width, p_count), jnp.bfloat16),
            pltpu.VMEM(occ_slots.shape, jnp.bfloat16),
            pltpu.SemaphoreType.DMA,
        ],
        compiler_params=params(),
        cost_estimate=cost(2 * three_center.size * width, 6 * three_center.size),
    )(half, in_hbm(occ_slots))

    pieces = ri_count // ao_count
    other_first, other_second = to_other_core(dressed_first), to_other_core(dressed_second)
    partial = product(dressed_first, other_first, first_all, pieces)
    partial = product(dressed_second, other_second, second_all, pieces, partial)
    partial = partial.reshape(ri_count, p_count // pieces, p_count)
    summed = spread(partial).sum(axis=0)
    moves = []
    for held in range(CORES * X_SIZE):
        holder, column = held // X_SIZE, held % X_SIZE
        for j in range(pieces):
            for x in range(X_SIZE):
                for core in range(CORES):
                    source = (held * pieces + j) * ao_count + x * CORES + core
                    row = (x * CORES + holder) * pieces + j
                    moves.append((source, row * ao_count + column * CORES + core))
    return lax.ppermute(summed, ("ri", "ao"), moves)


def solution(mesh):
    placed = (P("ao", "ri", None), P(), P(), P("ao", None), P("ao", None))
    return jax.shard_map(
        shards, mesh=mesh, in_specs=placed, out_specs=P("ri", "ao"), check_vma=False
    )
```

```python
import jax
import jax.numpy as jnp
from jax import lax
from jax.experimental import pallas as pl
from jax.experimental.pallas import tpu as pltpu
from jax.sharding import PartitionSpec as P

AO_ATOM = 32
RI_ATOM = 64
X_SIZE = 4
CORES = 2
SHIFTS = (0, 1, X_SIZE - 1, 2)
PARTS = 2
VMEM_LIMIT = 30 * 1024 * 1024
SEND_GROUP = 8
GROUP_SIGS = 2
NT = (((1,), (1,)), ((), ()))
TN = (((0,), (0,)), ((), ()))
VMEM = pl.BlockSpec(memory_space=pltpu.VMEM)
HBM = pl.BlockSpec(memory_space=pltpu.HBM)


def position():
    index = lax.axis_index("ao")
    return index // CORES, index % CORES


def dot(left, right, dims=(((1,), (0,)), ((), ()))):
    return lax.dot_general(left, right, dims, preferred_element_type=jnp.float32)


def screened_rows(refs, rows, own):
    order_hbm, mask_hbm, tensor_hbm, order_ref, mask_ref, tensor_ref, sems = refs
    p_count, row_count, width = tensor_ref.shape
    atoms = mask_ref.shape[2]
    group = 16
    copies = [
        pltpu.make_async_copy(order_hbm, order_ref, sems.at[0]),
        pltpu.make_async_copy(mask_hbm, mask_ref, sems.at[1]),
    ]
    for block in range(p_count // group):
        span = pl.ds(block * group, group)
        copies.append(
            pltpu.make_async_copy(tensor_hbm.at[span], tensor_ref.at[span], sems.at[2 + block])
        )
    for copy in copies:
        copy.start()
    lane = lax.broadcasted_iota(jnp.int32, (atoms, width), 1)
    spread = (lane // AO_ATOM == lax.broadcasted_iota(jnp.int32, (atoms, width), 0)).astype(
        jnp.bfloat16
    )
    copies[0].wait()
    copies[1].wait()
    atom = order_ref[(lax.axis_index("ri") * row_count) // AO_ATOM]
    x, core = position()
    holder = core if own else 1 - core
    first_ri_atom = ((x * CORES + holder) * p_count) // RI_ATOM
    masks = []
    for ri_atom in range(p_count // RI_ATOM):
        tiles = mask_ref[first_ri_atom + ri_atom, pl.ds(atom, 1), :].astype(jnp.float32)
        tiles = jnp.broadcast_to(tiles.astype(jnp.bfloat16), (8, atoms))
        masks.append(dot(tiles, spread)[:1].astype(jnp.bfloat16))
    for block in range(p_count // group):
        copies[2 + block].wait()
        span = pl.ds(block * group, group)
        by_rows = jnp.swapaxes(tensor_ref[span], 0, 1)
        rows[:, span, :] = by_rows * masks[block * group // RI_ATOM][None]


def place_pair(turned, row, columns):
    p_count = columns.shape[1] // CORES
    core = position()[1]
    for at, holder in ((0, core), (1, 1 - core)):
        span = pl.ds(pl.multiple_of(holder * p_count, p_count), p_count)
        turned[row, :, span] = columns[:, at * p_count : (at + 1) * p_count]


def send_sigs(turn, turned, send, sems, out_ref):
    ri_count, sig_count, row_count, p_count = send.shape
    for row in range(row_count):
        place_pair(turned, row, turn(row))
    step = 2
    copies = []
    for r in range(0, ri_count, step):
        block = turned[:, r * sig_count : (r + step) * sig_count, :]
        send[r : r + step] = jnp.swapaxes(block, 0, 1).reshape(step, sig_count, row_count, p_count)
        if (r + step) % SEND_GROUP == 0:
            blocks = pl.ds(r + step - SEND_GROUP, SEND_GROUP)
            copy = pltpu.make_async_copy(send.at[blocks], out_ref.at[blocks], sems.at[len(copies)])
            copy.start()
            copies.append(copy)
    for copy in copies:
        copy.wait()


def place_greens(own_ref, other_ref, greens):
    x, core = position()
    for k, shift in enumerate(SHIFTS):
        source = (x + X_SIZE - shift) % X_SIZE * CORES
        greens[source + core] = own_ref[k]
        greens[source + 1 - core] = other_ref[k]


def sigs_of_core(width):
    half = width // CORES
    return pl.ds(pl.multiple_of(position()[1] * half, half), half)


def rows_kernel(own, *refs):
    screened_rows(refs[:3] + refs[4:], refs[3], own)


def half_kernel(rows_ref, other_rows_ref, own_ref, other_ref, *refs):
    out_ref, kept_ref, other_kept_ref, greens, turned, send, sems, kept_sems = refs
    keep = [
        pltpu.make_async_copy(rows_ref, kept_ref, kept_sems.at[0]),
        pltpu.make_async_copy(other_rows_ref, other_kept_ref, kept_sems.at[1]),
    ]
    for copy in keep:
        copy.start()
    place_greens(own_ref, other_ref, greens)
    width = greens.shape[2]
    virt_t = greens[:, :, sigs_of_core(width)].reshape(width, -1).T

    def turn(row):
        pair = jnp.concatenate([rows_ref[row], other_rows_ref[row]], axis=0)
        return dot(virt_t, pair, NT).astype(jnp.bfloat16)

    send_sigs(turn, turned, send, sems, out_ref)
    for copy in keep:
        copy.wait()


def screen_kernel(rows_ref, other_rows_ref, out_ref, turned, send, sems):
    span = sigs_of_core(rows_ref.shape[2])

    def turn(row):
        pair = [ref[row, :, span] for ref in (rows_ref, other_rows_ref)]
        return jnp.concatenate(pair, axis=0).T

    send_sigs(turn, turned, send, sems, out_ref)


def occ_kernel(order_ref, own_ref, other_ref, occ_ref, greens):
    place_greens(own_ref, other_ref, greens)
    width = greens.shape[2]
    occ = greens[...].reshape(width, width)
    lane = lax.broadcasted_iota(jnp.int32, (AO_ATOM, width), 1)
    inner = lax.broadcasted_iota(jnp.int32, (AO_ATOM, width), 0)
    picks = [
        (lane == inner + order_ref[slot] * AO_ATOM).astype(jnp.bfloat16)
        for slot in range(width // AO_ATOM)
    ]
    pick = jnp.concatenate(picks, axis=0)
    by_nu = dot(pick, occ, NT).astype(jnp.bfloat16)
    occ_ref[...] = dot(by_nu, pick, NT).astype(jnp.bfloat16)


def dress_sigs(first_sig, half_ref, occ_ref, dressed_ref):
    sig_count, width, p_count = dressed_ref.shape
    for sig in range(sig_count):
        block = half_ref[:, first_sig + sig].reshape(width, p_count)
        dressed_ref[sig] = dot(occ_ref[...], block).astype(jnp.bfloat16)


def first_dress_kernel(half_ref, occ_hbm, dressed_ref, occ_ref, sem):
    copy = pltpu.make_async_copy(occ_hbm, occ_ref, sem)
    copy.start()
    copy.wait()
    dress_sigs(0, half_ref, occ_ref, dressed_ref)


def far_kernel(after_ref, before_ref, low_ref, high_ref):
    half = low_ref.shape[1]
    low_ref[...] = after_ref[:, :half]
    high_ref[...] = before_ref[:, half:]


def write_sums(total, positions, out_refs):
    x, core = position()
    rows, p_count = out_refs[0].shape[1], out_refs[0].shape[3]
    for out_ref, holder in zip(out_refs, (core, 1 - core)):
        span = pl.ds(pl.multiple_of(holder * p_count, p_count), p_count)
        for k, place in enumerate(positions):
            column = (x + X_SIZE - SHIFTS[place]) % X_SIZE
            for at in range(CORES):
                first = (k * CORES + at) * p_count
                part = total[span, first : first + p_count].T
                out_ref[column * CORES + at] = part.reshape(rows, p_count // rows, p_count)


def near_kernel(screened_hbm, *refs):
    blocks, (own_ref, other_ref, screened_ref, held, total, sems) = refs[:-6], refs[-6:]
    sig_count, places, width, chip_count = held.shape
    groups = []
    for at in range(0, sig_count, GROUP_SIGS):
        part, first = divmod(at, sig_count // PARTS)
        span = pl.ds(at, GROUP_SIGS)
        moves = [(screened_hbm.at[:, span], screened_ref.at[:, span])]
        for place in range(places):
            source = blocks[part * places + place].at[pl.ds(first, GROUP_SIGS)]
            moves.append((source, held.at[span, place]))
        copies = [
            pltpu.make_async_copy(*move, sems.at[at // GROUP_SIGS, index])
            for index, move in enumerate(moves)
        ]
        for copy in copies:
            copy.start()
        groups.append((at, copies))
    for out_ref in (own_ref, other_ref):
        out_ref[...] = jnp.zeros_like(out_ref)
    for at, copies in groups:
        for copy in copies:
            copy.wait()
        span = range(at, at + GROUP_SIGS)
        left = [screened_ref[:, sig].reshape(width, chip_count) for sig in span]
        left = jnp.concatenate(left, axis=0)
        for place in range(places):
            right = jnp.concatenate([held[sig, place] for sig in span], axis=0)
            columns = slice(place * chip_count, (place + 1) * chip_count)
            part = dot(left, right, TN)
            if at == 0:
                total[:, columns] = part
            else:
                total[:, columns] += part
    write_sums(total, range(places), (own_ref, other_ref))


def far_sum_kernel(screened_ref, near_own_ref, near_other_ref, *refs):
    blocks, (own_ref, other_ref, total) = refs[:-3], refs[-3:]
    own_ref[...] = near_own_ref[...]
    other_ref[...] = near_other_ref[...]
    ri_count, sig_count, row_count, chip_count = screened_ref.shape
    part_sigs = sig_count // PARTS
    for part in range(PARTS):
        low, high = blocks[2 * part : 2 * part + 2]
        left, right = [], []
        for sig in range(part_sigs):
            block = screened_ref[:, part * part_sigs + sig]
            left.append(block.reshape(ri_count * row_count, chip_count))
            right += [low[sig], high[sig]]
        sums = dot(jnp.concatenate(left, axis=0), jnp.concatenate(right, axis=0), TN)
        if part == 0:
            total[...] = sums
        else:
            total[...] += sums
    write_sums(total, (X_SIZE - 1,), (own_ref, other_ref))


def in_hbm(array):
    return pltpu.with_memory_space_constraint(array, pltpu.HBM)


def params():
    return pltpu.CompilerParams(vmem_limit_bytes=VMEM_LIMIT)


def cost(flops, touched):
    return pl.CostEstimate(flops=flops, bytes_accessed=touched, transcendentals=0)


def product(screened, near, far, p_count, rows):
    ri_count, sig_count, row_count, chip_count = screened.shape
    width = ri_count * row_count
    sums = jax.ShapeDtypeStruct((CORES * X_SIZE, rows, p_count // rows, p_count), jnp.float32)
    places = len(near[0])
    flops = 2 * chip_count * screened.size
    operands = [in_hbm(block) for part in near for block in part]
    own, other, screened = pl.pallas_call(
        near_kernel,
        in_specs=[HBM] * (1 + len(operands)),
        out_specs=[VMEM] * 3,
        out_shape=[sums, sums, jax.ShapeDtypeStruct(screened.shape, screened.dtype)],
        scratch_shapes=[
            pltpu.VMEM((sig_count, places, width, chip_count), jnp.bfloat16),
            pltpu.VMEM((chip_count, places * chip_count), jnp.float32),
            pltpu.SemaphoreType.DMA((sig_count // GROUP_SIGS, 1 + places)),
        ],
        compiler_params=params(),
        cost_estimate=cost(places * flops, 8 * screened.size),
    )(in_hbm(screened), *operands)
    operands = [block for part in far for block in part]
    return pl.pallas_call(
        far_sum_kernel,
        in_specs=[VMEM] * (3 + len(operands)),
        out_specs=[VMEM, VMEM],
        out_shape=[sums, sums],
        scratch_shapes=[pltpu.VMEM((chip_count, chip_count), jnp.float32)],
        compiler_params=params(),
        cost_estimate=cost(flops, 4 * screened.size),
    )(screened, own, other, *operands)


def shards(three_center, tile_mask, atom_order, green_occ, green_virt):
    p_count, row_count, width = three_center.shape
    ri_count, ao_count = lax.axis_size("ri"), lax.axis_size("ao")
    sig_count = width // ri_count // CORES
    chip_count = CORES * p_count

    def spread(block):
        return lax.all_to_all(block, "ri", split_axis=0, concat_axis=0, tiled=True)

    def to_other_core(block):
        return lax.ppermute(block, "ao", [(i, i ^ 1) for i in range(ao_count)])

    def along_x(block, shift):
        moves = [(i, (i + CORES * shift) % ao_count) for i in range(ao_count)]
        return lax.ppermute(block, "ao", moves)

    def along_x_all(block):
        return [block] + [along_x(block, shift) for shift in SHIFTS[1:]]

    def to_both_cores(blocks):
        own = jnp.stack(blocks)
        return own, to_other_core(own)

    def far_blocks(after, before, weight):
        half = jax.ShapeDtypeStruct((after.shape[0], width // 2, chip_count), jnp.bfloat16)
        low, high = pl.pallas_call(
            far_kernel,
            in_specs=[VMEM, VMEM],
            out_specs=[VMEM, VMEM],
            out_shape=[half, half],
            compiler_params=params(),
            cost_estimate=cost(weight, 4 * after.size),
        )(after, before)
        return [along_x(low, 1), along_x(high, -1)]

    other_center = to_other_core(three_center)
    rows_shape = jax.ShapeDtypeStruct((row_count, p_count, width), jnp.bfloat16)

    def screened_by_rows(own):
        return pl.pallas_call(
            lambda *refs: rows_kernel(own, *refs),
            in_specs=[HBM] * 3,
            out_specs=VMEM,
            out_shape=rows_shape,
            scratch_shapes=[
                pltpu.SMEM(atom_order.shape, jnp.int32),
                pltpu.VMEM(tile_mask.shape, jnp.int32),
                pltpu.VMEM(three_center.shape, jnp.bfloat16),
                pltpu.SemaphoreType.DMA((2 + p_count // 16,)),
            ],
            compiler_params=params(),
            cost_estimate=cost(10**9, 4 * three_center.size),
        )(in_hbm(atom_order), in_hbm(tile_mask), in_hbm(three_center) if own else other_center)

    virt, own_rows = lax.optimization_barrier((along_x_all(green_virt), screened_by_rows(True)))
    greens_scratch = pltpu.VMEM((ao_count, *green_virt.shape), jnp.bfloat16)
    send_scratch = [
        pltpu.VMEM((row_count, width // CORES, chip_count), jnp.bfloat16),
        pltpu.VMEM((ri_count, sig_count, row_count, chip_count), jnp.bfloat16),
        pltpu.SemaphoreType.DMA((ri_count // SEND_GROUP,)),
    ]
    send_shape = pltpu.HBM((ri_count, sig_count, row_count, chip_count), jnp.bfloat16)
    kept_shape = pltpu.HBM(rows_shape.shape, jnp.bfloat16)
    send_half, *kept_rows = pl.pallas_call(
        half_kernel,
        in_specs=[VMEM] * 4,
        out_specs=[HBM] * 3,
        out_shape=[send_shape, kept_shape, kept_shape],
        scratch_shapes=[greens_scratch] + send_scratch + [pltpu.SemaphoreType.DMA((CORES,))],
        compiler_params=params(),
        cost_estimate=cost(2 * three_center.size * width, 6 * three_center.size),
    )(own_rows, screened_by_rows(False), *to_both_cores(virt))
    half = spread(send_half)

    occ = pl.pallas_call(
        occ_kernel,
        in_specs=[pl.BlockSpec(memory_space=pltpu.SMEM), VMEM, VMEM],
        out_specs=VMEM,
        out_shape=jax.ShapeDtypeStruct((width, width), jnp.bfloat16),
        scratch_shapes=[greens_scratch],
        compiler_params=params(),
        cost_estimate=cost(4 * width**3, 8 * width * width),
    )(atom_order, *to_both_cores(along_x_all(green_occ)))
    send_screened = pl.pallas_call(
        screen_kernel,
        in_specs=[VMEM] * 2,
        out_specs=HBM,
        out_shape=send_shape,
        scratch_shapes=send_scratch,
        compiler_params=params(),
        cost_estimate=cost(0, 6 * three_center.size),
    )(*kept_rows)

    half, send_screened, occ = lax.optimization_barrier((half, send_screened, occ))
    screened = spread(send_screened)
    dressed_shape = jax.ShapeDtypeStruct((sig_count // PARTS, width, chip_count), jnp.bfloat16)
    dress_cost = cost(half.size * width, 3 * half.size)
    first_dressed, occ = pl.pallas_call(
        first_dress_kernel,
        in_specs=[VMEM, HBM],
        out_specs=[VMEM, VMEM],
        out_shape=[dressed_shape, jax.ShapeDtypeStruct(occ.shape, jnp.bfloat16)],
        scratch_shapes=[pltpu.SemaphoreType.DMA],
        compiler_params=params(),
        cost_estimate=dress_cost,
    )(half, in_hbm(occ))
    second_dressed = pl.pallas_call(
        lambda *refs: dress_sigs(sig_count // PARTS, *refs),
        in_specs=[VMEM, VMEM],
        out_specs=VMEM,
        out_shape=dressed_shape,
        compiler_params=params(),
        cost_estimate=dress_cost,
    )(half, occ)

    near, far = [], []
    for block, weight in ((first_dressed, 10**12), (second_dressed, 10**6)):
        after, before = along_x(block, 1), along_x(block, -1)
        near.append([block, after, before])
        far.append(far_blocks(after, before, weight))
    rows = ri_count // ao_count
    own, other = product(screened, near, far, p_count, rows)
    partial = own + to_other_core(other)
    return spread(partial.reshape(ri_count, p_count // rows, p_count)).sum(axis=0)


def solution(mesh):
    placed = (P("ao", "ri", None), P(), P(), P("ao", None), P("ao", None))
    return jax.shard_map(
        shards, mesh=mesh, in_specs=placed, out_specs=P("ri", "ao"), check_vma=False
    )
```

```python
import jax
import jax.numpy as jnp
from jax import lax
from jax.experimental import pallas as pl
from jax.experimental.pallas import tpu as pltpu
from jax.sharding import PartitionSpec as P

AO_ATOM = 32
RI_ATOM = 64
X_SIZE = 4
CORES = 2
SHIFTS = (0, 1, X_SIZE - 1, 2)
PARTS = 2
VMEM_LIMIT = 30 * 1024 * 1024
SEND_GROUP = 8
GROUP_SIGS = 2
NT = (((1,), (1,)), ((), ()))
TN = (((0,), (0,)), ((), ()))
VMEM = pl.BlockSpec(memory_space=pltpu.VMEM)
HBM = pl.BlockSpec(memory_space=pltpu.HBM)


def position():
    index = lax.axis_index("ao")
    return index // CORES, index % CORES


def dot(left, right, dims=(((1,), (0,)), ((), ()))):
    return lax.dot_general(left, right, dims, preferred_element_type=jnp.float32)


def screened_rows(refs, rows, own):
    order_hbm, mask_hbm, tensor_hbm, order_ref, mask_ref, tensor_ref, sems = refs
    p_count, row_count, width = tensor_ref.shape
    atoms = mask_ref.shape[2]
    group = 16
    copies = [
        pltpu.make_async_copy(order_hbm, order_ref, sems.at[0]),
        pltpu.make_async_copy(mask_hbm, mask_ref, sems.at[1]),
    ]
    for block in range(p_count // group):
        span = pl.ds(block * group, group)
        copies.append(
            pltpu.make_async_copy(tensor_hbm.at[span], tensor_ref.at[span], sems.at[2 + block])
        )
    for copy in copies:
        copy.start()
    lane = lax.broadcasted_iota(jnp.int32, (atoms, width), 1)
    spread = (lane // AO_ATOM == lax.broadcasted_iota(jnp.int32, (atoms, width), 0)).astype(
        jnp.bfloat16
    )
    copies[0].wait()
    copies[1].wait()
    atom = order_ref[(lax.axis_index("ri") * row_count) // AO_ATOM]
    x, core = position()
    holder = core if own else 1 - core
    first_ri_atom = ((x * CORES + holder) * p_count) // RI_ATOM
    masks = []
    for ri_atom in range(p_count // RI_ATOM):
        tiles = mask_ref[first_ri_atom + ri_atom, pl.ds(atom, 1), :].astype(jnp.float32)
        tiles = jnp.broadcast_to(tiles.astype(jnp.bfloat16), (8, atoms))
        masks.append(dot(tiles, spread)[:1].astype(jnp.bfloat16))
    for block in range(p_count // group):
        copies[2 + block].wait()
        span = pl.ds(block * group, group)
        by_rows = jnp.swapaxes(tensor_ref[span], 0, 1)
        rows[:, span, :] = by_rows * masks[block * group // RI_ATOM][None]


def place_pair(turned, row, columns):
    p_count = columns.shape[1] // CORES
    core = position()[1]
    for at, holder in ((0, core), (1, 1 - core)):
        span = pl.ds(pl.multiple_of(holder * p_count, p_count), p_count)
        turned[row, :, span] = columns[:, at * p_count : (at + 1) * p_count]


def send_sigs(turn, turned, send, sems, out_ref):
    ri_count, sig_count, _, row_count, p_count = send.shape
    for row in range(row_count):
        place_pair(turned, row, turn(row))
    step = 2
    copies = []
    for r in range(0, ri_count, step):
        block = turned[:, r * sig_count : (r + step) * sig_count, :]
        block = jnp.swapaxes(block, 0, 1)
        for core in range(CORES):
            part = block[:, :, core * p_count : (core + 1) * p_count]
            send[r : r + step, :, core] = part.reshape(step, sig_count, row_count, p_count)
        if (r + step) % SEND_GROUP == 0:
            blocks = pl.ds(r + step - SEND_GROUP, SEND_GROUP)
            copy = pltpu.make_async_copy(send.at[blocks], out_ref.at[blocks], sems.at[len(copies)])
            copy.start()
            copies.append(copy)
    for copy in copies:
        copy.wait()


def place_greens(own_ref, other_ref, greens):
    x, core = position()
    for k, shift in enumerate(SHIFTS):
        source = (x + X_SIZE - shift) % X_SIZE * CORES
        greens[source + core] = own_ref[k]
        greens[source + 1 - core] = other_ref[k]


def sigs_of_core(width):
    half = width // CORES
    return pl.ds(pl.multiple_of(position()[1] * half, half), half)


def rows_kernel(own, *refs):
    screened_rows(refs[:3] + refs[4:], refs[3], own)


def half_kernel(rows_ref, other_rows_ref, own_ref, other_ref, *refs):
    out_ref, kept_ref, other_kept_ref, greens, turned, send, sems, kept_sems = refs
    keep = [
        pltpu.make_async_copy(rows_ref, kept_ref, kept_sems.at[0]),
        pltpu.make_async_copy(other_rows_ref, other_kept_ref, kept_sems.at[1]),
    ]
    for copy in keep:
        copy.start()
    place_greens(own_ref, other_ref, greens)
    width = greens.shape[2]
    virt_t = greens[:, :, sigs_of_core(width)].reshape(width, -1).T

    def turn(row):
        pair = jnp.concatenate([rows_ref[row], other_rows_ref[row]], axis=0)
        return dot(virt_t, pair, NT).astype(jnp.bfloat16)

    send_sigs(turn, turned, send, sems, out_ref)
    for copy in keep:
        copy.wait()


def screen_kernel(rows_ref, other_rows_ref, out_ref, turned, send, sems):
    span = sigs_of_core(rows_ref.shape[2])

    def turn(row):
        pair = [ref[row, :, span] for ref in (rows_ref, other_rows_ref)]
        return jnp.concatenate(pair, axis=0).T

    send_sigs(turn, turned, send, sems, out_ref)


def occ_kernel(order_ref, own_ref, other_ref, occ_ref, greens):
    place_greens(own_ref, other_ref, greens)
    width = greens.shape[2]
    occ = greens[...].reshape(width, width)
    lane = lax.broadcasted_iota(jnp.int32, (AO_ATOM, width), 1)
    inner = lax.broadcasted_iota(jnp.int32, (AO_ATOM, width), 0)
    picks = [
        (lane == inner + order_ref[slot] * AO_ATOM).astype(jnp.bfloat16)
        for slot in range(width // AO_ATOM)
    ]
    pick = jnp.concatenate(picks, axis=0)
    by_nu = dot(pick, occ, NT).astype(jnp.bfloat16)
    occ_ref[...] = dot(by_nu, pick, NT).astype(jnp.bfloat16)


def at_sig(ref, sig):
    parts = [ref[:, sig, core] for core in range(CORES)]
    return jnp.concatenate([part.reshape(-1, part.shape[2]) for part in parts], axis=1)


def dress_sigs(first_sig, half_ref, occ_ref, dressed_ref):
    for sig in range(dressed_ref.shape[0]):
        block = at_sig(half_ref, first_sig + sig)
        dressed_ref[sig] = dot(occ_ref[...], block).astype(jnp.bfloat16)


def first_dress_kernel(half_ref, occ_hbm, dressed_ref, occ_ref, sem):
    copy = pltpu.make_async_copy(occ_hbm, occ_ref, sem)
    copy.start()
    copy.wait()
    dress_sigs(0, half_ref, occ_ref, dressed_ref)


def far_kernel(after_ref, before_ref, low_ref, high_ref):
    half = low_ref.shape[1]
    low_ref[...] = after_ref[:, :half]
    high_ref[...] = before_ref[:, half:]


def write_sums(total, positions, out_refs):
    x, core = position()
    rows, p_count = out_refs[0].shape[1], out_refs[0].shape[3]
    for out_ref, holder in zip(out_refs, (core, 1 - core)):
        span = pl.ds(pl.multiple_of(holder * p_count, p_count), p_count)
        for k, place in enumerate(positions):
            column = (x + X_SIZE - SHIFTS[place]) % X_SIZE
            for at in range(CORES):
                first = (k * CORES + at) * p_count
                part = total[span, first : first + p_count].T
                out_ref[column * CORES + at] = part.reshape(rows, p_count // rows, p_count)


def near_kernel(screened_hbm, *refs):
    blocks, (own_ref, other_ref, screened_ref, held, total, sems) = refs[:-6], refs[-6:]
    sig_count, places, width, chip_count = held.shape
    groups = []
    for at in range(0, sig_count, GROUP_SIGS):
        part, first = divmod(at, sig_count // PARTS)
        span = pl.ds(at, GROUP_SIGS)
        moves = [(screened_hbm.at[:, span], screened_ref.at[:, span])]
        for place in range(places):
            source = blocks[part * places + place].at[pl.ds(first, GROUP_SIGS)]
            moves.append((source, held.at[span, place]))
        copies = [
            pltpu.make_async_copy(*move, sems.at[at // GROUP_SIGS, index])
            for index, move in enumerate(moves)
        ]
        for copy in copies:
            copy.start()
        groups.append((at, copies))
    for out_ref in (own_ref, other_ref):
        out_ref[...] = jnp.zeros_like(out_ref)
    for at, copies in groups:
        for copy in copies:
            copy.wait()
        span = range(at, at + GROUP_SIGS)
        left = jnp.concatenate([at_sig(screened_ref, sig) for sig in span], axis=0)
        for place in range(places):
            right = jnp.concatenate([held[sig, place] for sig in span], axis=0)
            columns = slice(place * chip_count, (place + 1) * chip_count)
            part = dot(left, right, TN)
            if at == 0:
                total[:, columns] = part
            else:
                total[:, columns] += part
    write_sums(total, range(places), (own_ref, other_ref))


def far_sum_kernel(screened_ref, near_own_ref, near_other_ref, *refs):
    blocks, (own_ref, other_ref, total) = refs[:-3], refs[-3:]
    own_ref[...] = near_own_ref[...]
    other_ref[...] = near_other_ref[...]
    part_sigs = screened_ref.shape[1] // PARTS
    for part in range(PARTS):
        low, high = blocks[2 * part : 2 * part + 2]
        left, right = [], []
        for sig in range(part_sigs):
            left.append(at_sig(screened_ref, part * part_sigs + sig))
            right += [low[sig], high[sig]]
        sums = dot(jnp.concatenate(left, axis=0), jnp.concatenate(right, axis=0), TN)
        if part == 0:
            total[...] = sums
        else:
            total[...] += sums
    write_sums(total, (X_SIZE - 1,), (own_ref, other_ref))


def in_hbm(array):
    return pltpu.with_memory_space_constraint(array, pltpu.HBM)


def params():
    return pltpu.CompilerParams(vmem_limit_bytes=VMEM_LIMIT)


def cost(flops, touched):
    return pl.CostEstimate(flops=flops, bytes_accessed=touched, transcendentals=0)


def product(screened, near, far, p_count, rows):
    ri_count, sig_count, _, row_count, _ = screened.shape
    width, chip_count = ri_count * row_count, CORES * p_count
    sums = jax.ShapeDtypeStruct((CORES * X_SIZE, rows, p_count // rows, p_count), jnp.float32)
    places = len(near[0])
    flops = 2 * chip_count * screened.size
    operands = [in_hbm(block) for part in near for block in part]
    own, other, screened = pl.pallas_call(
        near_kernel,
        in_specs=[HBM] * (1 + len(operands)),
        out_specs=[VMEM] * 3,
        out_shape=[sums, sums, jax.ShapeDtypeStruct(screened.shape, screened.dtype)],
        scratch_shapes=[
            pltpu.VMEM((sig_count, places, width, chip_count), jnp.bfloat16),
            pltpu.VMEM((chip_count, places * chip_count), jnp.float32),
            pltpu.SemaphoreType.DMA((sig_count // GROUP_SIGS, 1 + places)),
        ],
        compiler_params=params(),
        cost_estimate=cost(places * flops, 8 * screened.size),
    )(in_hbm(screened), *operands)
    operands = [block for part in far for block in part]
    return pl.pallas_call(
        far_sum_kernel,
        in_specs=[VMEM] * (3 + len(operands)),
        out_specs=[VMEM, VMEM],
        out_shape=[sums, sums],
        scratch_shapes=[pltpu.VMEM((chip_count, chip_count), jnp.float32)],
        compiler_params=params(),
        cost_estimate=cost(flops, 4 * screened.size),
    )(screened, own, other, *operands)


def shards(three_center, tile_mask, atom_order, green_occ, green_virt):
    p_count, row_count, width = three_center.shape
    ri_count, ao_count = lax.axis_size("ri"), lax.axis_size("ao")
    sig_count = width // ri_count // CORES
    chip_count = CORES * p_count

    def spread(block):
        return lax.all_to_all(block, "ri", split_axis=0, concat_axis=0, tiled=True)

    def to_other_core(block):
        return lax.ppermute(block, "ao", [(i, i ^ 1) for i in range(ao_count)])

    def along_x(block, shift):
        moves = [(i, (i + CORES * shift) % ao_count) for i in range(ao_count)]
        return lax.ppermute(block, "ao", moves)

    def along_x_all(block):
        return [block] + [along_x(block, shift) for shift in SHIFTS[1:]]

    def to_both_cores(blocks):
        own = jnp.stack(blocks)
        return own, to_other_core(own)

    def far_blocks(after, before, weight):
        half = jax.ShapeDtypeStruct((after.shape[0], width // 2, chip_count), jnp.bfloat16)
        low, high = pl.pallas_call(
            far_kernel,
            in_specs=[VMEM, VMEM],
            out_specs=[VMEM, VMEM],
            out_shape=[half, half],
            compiler_params=params(),
            cost_estimate=cost(weight, 4 * after.size),
        )(after, before)
        return [along_x(low, 1), along_x(high, -1)]

    other_center = to_other_core(three_center)
    rows_shape = jax.ShapeDtypeStruct((row_count, p_count, width), jnp.bfloat16)

    def screened_by_rows(own):
        return pl.pallas_call(
            lambda *refs: rows_kernel(own, *refs),
            in_specs=[HBM] * 3,
            out_specs=VMEM,
            out_shape=rows_shape,
            scratch_shapes=[
                pltpu.SMEM(atom_order.shape, jnp.int32),
                pltpu.VMEM(tile_mask.shape, jnp.int32),
                pltpu.VMEM(three_center.shape, jnp.bfloat16),
                pltpu.SemaphoreType.DMA((2 + p_count // 16,)),
            ],
            compiler_params=params(),
            cost_estimate=cost(10**9, 4 * three_center.size),
        )(in_hbm(atom_order), in_hbm(tile_mask), in_hbm(three_center) if own else other_center)

    virt, rows = lax.optimization_barrier(
        (along_x_all(green_virt), [screened_by_rows(True), screened_by_rows(False)])
    )
    greens_scratch = pltpu.VMEM((ao_count, *green_virt.shape), jnp.bfloat16)
    send_scratch = [
        pltpu.VMEM((row_count, width // CORES, chip_count), jnp.bfloat16),
        pltpu.VMEM((ri_count, sig_count, CORES, row_count, p_count), jnp.bfloat16),
        pltpu.SemaphoreType.DMA((ri_count // SEND_GROUP,)),
    ]
    send_shape = pltpu.HBM((ri_count, sig_count, CORES, row_count, p_count), jnp.bfloat16)
    kept_shape = pltpu.HBM(rows_shape.shape, jnp.bfloat16)
    send_half, *kept_rows = pl.pallas_call(
        half_kernel,
        in_specs=[VMEM] * 4,
        out_specs=[HBM] * 3,
        out_shape=[send_shape, kept_shape, kept_shape],
        scratch_shapes=[greens_scratch] + send_scratch + [pltpu.SemaphoreType.DMA((CORES,))],
        compiler_params=params(),
        cost_estimate=cost(2 * three_center.size * width, 6 * three_center.size),
    )(*rows, *to_both_cores(virt))
    half = spread(send_half)

    occ = pl.pallas_call(
        occ_kernel,
        in_specs=[pl.BlockSpec(memory_space=pltpu.SMEM), VMEM, VMEM],
        out_specs=VMEM,
        out_shape=jax.ShapeDtypeStruct((width, width), jnp.bfloat16),
        scratch_shapes=[greens_scratch],
        compiler_params=params(),
        cost_estimate=cost(4 * width**3, 8 * width * width),
    )(atom_order, *to_both_cores(along_x_all(green_occ)))
    send_screened = pl.pallas_call(
        screen_kernel,
        in_specs=[VMEM] * 2,
        out_specs=HBM,
        out_shape=send_shape,
        scratch_shapes=send_scratch,
        compiler_params=params(),
        cost_estimate=cost(0, 6 * three_center.size),
    )(*kept_rows)

    half, send_screened, occ = lax.optimization_barrier((half, send_screened, occ))
    screened = spread(send_screened)
    dressed_shape = jax.ShapeDtypeStruct((sig_count // PARTS, width, chip_count), jnp.bfloat16)
    dress_cost = cost(half.size * width, 3 * half.size)
    first_dressed, occ = pl.pallas_call(
        first_dress_kernel,
        in_specs=[VMEM, HBM],
        out_specs=[VMEM, VMEM],
        out_shape=[dressed_shape, jax.ShapeDtypeStruct(occ.shape, jnp.bfloat16)],
        scratch_shapes=[pltpu.SemaphoreType.DMA],
        compiler_params=params(),
        cost_estimate=dress_cost,
    )(half, in_hbm(occ))
    second_dressed = pl.pallas_call(
        lambda *refs: dress_sigs(sig_count // PARTS, *refs),
        in_specs=[VMEM, VMEM],
        out_specs=VMEM,
        out_shape=dressed_shape,
        compiler_params=params(),
        cost_estimate=dress_cost,
    )(half, occ)

    near, far = [], []
    for block, weight in ((first_dressed, 10**12), (second_dressed, 10**6)):
        after, before = along_x(block, 1), along_x(block, -1)
        near.append([block, after, before])
        far.append(far_blocks(after, before, weight))
    rows = ri_count // ao_count
    own, other = product(screened, near, far, p_count, rows)
    partial = own + to_other_core(other)
    return spread(partial.reshape(ri_count, p_count // rows, p_count)).sum(axis=0)


def solution(mesh):
    placed = (P("ao", "ri", None), P(), P(), P("ao", None), P("ao", None))
    return jax.shard_map(
        shards, mesh=mesh, in_specs=placed, out_specs=P("ri", "ao"), check_vma=False
    )
```

```python
import jax
import jax.numpy as jnp
from jax import lax
from jax.experimental import pallas as pl
from jax.experimental.pallas import tpu as pltpu
from jax.sharding import PartitionSpec as P

AO_ATOM = 32
RI_ATOM = 64
X_SIZE = 4
CORES = 2
SHIFTS = (0, 1, X_SIZE - 1, 2)
PARTS = 2
VMEM_LIMIT = 30 * 1024 * 1024
SEND_GROUP = 8
GROUP_SIGS = 2
NT = (((1,), (1,)), ((), ()))
TN = (((0,), (0,)), ((), ()))
VMEM = pl.BlockSpec(memory_space=pltpu.VMEM)
HBM = pl.BlockSpec(memory_space=pltpu.HBM)


def position():
    index = lax.axis_index("ao")
    return index // CORES, index % CORES


def dot(left, right, dims=(((1,), (0,)), ((), ()))):
    return lax.dot_general(left, right, dims, preferred_element_type=jnp.float32)


def screened_rows(refs, rows, own):
    order_hbm, mask_hbm, tensor_hbm, order_ref, mask_ref, tensor_ref, sems = refs
    p_count, row_count, width = tensor_ref.shape
    atoms = mask_ref.shape[2]
    group = 16
    copies = [
        pltpu.make_async_copy(order_hbm, order_ref, sems.at[0]),
        pltpu.make_async_copy(mask_hbm, mask_ref, sems.at[1]),
    ]
    for block in range(p_count // group):
        span = pl.ds(block * group, group)
        copies.append(
            pltpu.make_async_copy(tensor_hbm.at[span], tensor_ref.at[span], sems.at[2 + block])
        )
    for copy in copies:
        copy.start()
    lane = lax.broadcasted_iota(jnp.int32, (atoms, width), 1)
    spread = (lane // AO_ATOM == lax.broadcasted_iota(jnp.int32, (atoms, width), 0)).astype(
        jnp.bfloat16
    )
    copies[0].wait()
    copies[1].wait()
    atom = order_ref[(lax.axis_index("ri") * row_count) // AO_ATOM]
    x, core = position()
    holder = core if own else 1 - core
    first_ri_atom = ((x * CORES + holder) * p_count) // RI_ATOM
    masks = []
    for ri_atom in range(p_count // RI_ATOM):
        tiles = mask_ref[first_ri_atom + ri_atom, pl.ds(atom, 1), :].astype(jnp.float32)
        tiles = jnp.broadcast_to(tiles.astype(jnp.bfloat16), (8, atoms))
        masks.append(dot(tiles, spread)[:1].astype(jnp.bfloat16))
    for block in range(p_count // group):
        copies[2 + block].wait()
        span = pl.ds(block * group, group)
        by_rows = jnp.swapaxes(tensor_ref[span], 0, 1)
        rows[:, span, :] = by_rows * masks[block * group // RI_ATOM][None]


def place_pair(turned, row, columns):
    p_count = columns.shape[1] // CORES
    core = position()[1]
    for at, holder in ((0, core), (1, 1 - core)):
        span = pl.ds(pl.multiple_of(holder * p_count, p_count), p_count)
        turned[row, :, span] = columns[:, at * p_count : (at + 1) * p_count]


def send_sigs(turn, turned, send, sems, out_ref):
    ri_count, sig_count, _, row_count, p_count = send.shape
    for row in range(row_count):
        place_pair(turned, row, turn(row))
    step = 2
    copies = []
    for r in range(0, ri_count, step):
        block = turned[:, r * sig_count : (r + step) * sig_count, :]
        block = jnp.swapaxes(block, 0, 1)
        for core in range(CORES):
            part = block[:, :, core * p_count : (core + 1) * p_count]
            send[r : r + step, :, core] = part.reshape(step, sig_count, row_count, p_count)
        if (r + step) % SEND_GROUP == 0:
            blocks = pl.ds(r + step - SEND_GROUP, SEND_GROUP)
            copy = pltpu.make_async_copy(send.at[blocks], out_ref.at[blocks], sems.at[len(copies)])
            copy.start()
            copies.append(copy)
    for copy in copies:
        copy.wait()


def place_greens(own_ref, other_ref, greens):
    x, core = position()
    for k, shift in enumerate(SHIFTS):
        source = (x + X_SIZE - shift) % X_SIZE * CORES
        greens[source + core] = own_ref[k]
        greens[source + 1 - core] = other_ref[k]


def sigs_of_core(width):
    half = width // CORES
    return pl.ds(pl.multiple_of(position()[1] * half, half), half)


def rows_kernel(own, *refs):
    screened_rows(refs[:3] + refs[4:], refs[3], own)


def half_kernel(rows_ref, other_rows_ref, own_ref, other_ref, *refs):
    out_ref, kept_ref, other_kept_ref, greens, turned, send, sems, kept_sems = refs
    keep = [
        pltpu.make_async_copy(rows_ref, kept_ref, kept_sems.at[0]),
        pltpu.make_async_copy(other_rows_ref, other_kept_ref, kept_sems.at[1]),
    ]
    for copy in keep:
        copy.start()
    place_greens(own_ref, other_ref, greens)
    width = greens.shape[2]
    virt_t = greens[:, :, sigs_of_core(width)].reshape(width, -1).T

    def turn(row):
        pair = jnp.concatenate([rows_ref[row], other_rows_ref[row]], axis=0)
        return dot(virt_t, pair, NT).astype(jnp.bfloat16)

    send_sigs(turn, turned, send, sems, out_ref)
    for copy in keep:
        copy.wait()


def screen_kernel(rows_ref, other_rows_ref, out_ref, turned, send, sems):
    span = sigs_of_core(rows_ref.shape[2])

    def turn(row):
        pair = [ref[row, :, span] for ref in (rows_ref, other_rows_ref)]
        return jnp.concatenate(pair, axis=0).T

    send_sigs(turn, turned, send, sems, out_ref)


def occ_kernel(order_ref, own_ref, other_ref, occ_ref, greens):
    place_greens(own_ref, other_ref, greens)
    width = greens.shape[2]
    occ = greens[...].reshape(width, width)
    lane = lax.broadcasted_iota(jnp.int32, (AO_ATOM, width), 1)
    inner = lax.broadcasted_iota(jnp.int32, (AO_ATOM, width), 0)
    picks = [
        (lane == inner + order_ref[slot] * AO_ATOM).astype(jnp.bfloat16)
        for slot in range(width // AO_ATOM)
    ]
    pick = jnp.concatenate(picks, axis=0)
    by_nu = dot(pick, occ, NT).astype(jnp.bfloat16)
    occ_ref[...] = dot(by_nu, pick, NT).astype(jnp.bfloat16)


def at_sig(ref, sig):
    parts = [ref[:, sig, core] for core in range(CORES)]
    return jnp.concatenate([part.reshape(-1, part.shape[2]) for part in parts], axis=1)


def dress_sigs(first_sig, half_ref, occ_ref, dressed_ref):
    for sig in range(dressed_ref.shape[0]):
        block = at_sig(half_ref, first_sig + sig)
        dressed_ref[sig] = dot(occ_ref[...], block).astype(jnp.bfloat16)


def first_dress_kernel(half_ref, occ_hbm, dressed_ref, occ_ref, sem):
    copy = pltpu.make_async_copy(occ_hbm, occ_ref, sem)
    copy.start()
    copy.wait()
    dress_sigs(0, half_ref, occ_ref, dressed_ref)


def far_kernel(after_ref, before_ref, low_ref, high_ref):
    half = low_ref.shape[1]
    low_ref[...] = after_ref[:, :half]
    high_ref[...] = before_ref[:, half:]


def write_sums(total, positions, out_refs):
    x, core = position()
    rows, p_count = out_refs[0].shape[1], out_refs[0].shape[3]
    for out_ref, holder in zip(out_refs, (core, 1 - core)):
        span = pl.ds(pl.multiple_of(holder * p_count, p_count), p_count)
        for k, place in enumerate(positions):
            column = (x + X_SIZE - SHIFTS[place]) % X_SIZE
            for at in range(CORES):
                first = (k * CORES + at) * p_count
                part = total[span, first : first + p_count].T
                out_ref[column * CORES + at] = part.reshape(rows, p_count // rows, p_count)


def near_kernel(screened_hbm, *refs):
    blocks, (own_ref, other_ref, screened_ref, held, total, sems) = refs[:-6], refs[-6:]
    sig_count, places, width, chip_count = held.shape
    groups = []
    for at in range(0, sig_count, GROUP_SIGS):
        part, first = divmod(at, sig_count // PARTS)
        span = pl.ds(at, GROUP_SIGS)
        moves = [(screened_hbm.at[:, span], screened_ref.at[:, span])]
        for place in range(places):
            source = blocks[part * places + place].at[pl.ds(first, GROUP_SIGS)]
            moves.append((source, held.at[span, place]))
        copies = [
            pltpu.make_async_copy(*move, sems.at[at // GROUP_SIGS, index])
            for index, move in enumerate(moves)
        ]
        for copy in copies:
            copy.start()
        groups.append((at, copies))
    for out_ref in (own_ref, other_ref):
        out_ref[...] = jnp.zeros_like(out_ref)
    for at, copies in groups:
        for copy in copies:
            copy.wait()
        span = range(at, at + GROUP_SIGS)
        left = jnp.concatenate([at_sig(screened_ref, sig) for sig in span], axis=0)
        for place in range(places):
            right = jnp.concatenate([held[sig, place] for sig in span], axis=0)
            columns = slice(place * chip_count, (place + 1) * chip_count)
            part = dot(left, right, TN)
            if at == 0:
                total[:, columns] = part
            else:
                total[:, columns] += part
    write_sums(total, range(places), (own_ref, other_ref))


def far_sum_kernel(screened_ref, near_own_ref, near_crossed_ref, *refs):
    blocks, (own_ref, other_ref, total) = refs[:-3], refs[-3:]
    own_ref[...] = near_own_ref[...] + near_crossed_ref[...]
    part_sigs = screened_ref.shape[1] // PARTS
    for part in range(PARTS):
        low, high = blocks[2 * part : 2 * part + 2]
        left, right = [], []
        for sig in range(part_sigs):
            left.append(at_sig(screened_ref, part * part_sigs + sig))
            right += [low[sig], high[sig]]
        sums = dot(jnp.concatenate(left, axis=0), jnp.concatenate(right, axis=0), TN)
        if part == 0:
            total[...] = sums
        else:
            total[...] += sums
    core = position()[1]
    rows, p_count = own_ref.shape[1], own_ref.shape[3]
    for out_ref, first, holder in ((own_ref, far_block(), core), (other_ref, 0, 1 - core)):
        span = pl.ds(pl.multiple_of(holder * p_count, p_count), p_count)
        for at in range(CORES):
            part = total[span, at * p_count : (at + 1) * p_count].T
            out_ref[first + at] = part.reshape(rows, p_count // rows, p_count)


def far_block():
    return (position()[0] + X_SIZE - SHIFTS[-1]) % X_SIZE * CORES


def in_hbm(array):
    return pltpu.with_memory_space_constraint(array, pltpu.HBM)


def params():
    return pltpu.CompilerParams(vmem_limit_bytes=VMEM_LIMIT)


def cost(flops, touched):
    return pl.CostEstimate(flops=flops, bytes_accessed=touched, transcendentals=0)


def product(screened, near, far, p_count, rows, to_other_core):
    ri_count, sig_count, _, row_count, _ = screened.shape
    width, chip_count = ri_count * row_count, CORES * p_count
    sums = jax.ShapeDtypeStruct((CORES * X_SIZE, rows, p_count // rows, p_count), jnp.float32)
    places = len(near[0])
    flops = 2 * chip_count * screened.size
    operands = [in_hbm(block) for part in near for block in part]
    own, other, screened = pl.pallas_call(
        near_kernel,
        in_specs=[HBM] * (1 + len(operands)),
        out_specs=[VMEM] * 3,
        out_shape=[sums, sums, jax.ShapeDtypeStruct(screened.shape, screened.dtype)],
        scratch_shapes=[
            pltpu.VMEM((sig_count, places, width, chip_count), jnp.bfloat16),
            pltpu.VMEM((chip_count, places * chip_count), jnp.float32),
            pltpu.SemaphoreType.DMA((sig_count // GROUP_SIGS, 1 + places)),
        ],
        compiler_params=params(),
        cost_estimate=cost(places * flops, 8 * screened.size),
    )(in_hbm(screened), *operands)
    operands = [block for part in far for block in part]
    far_sums = jax.ShapeDtypeStruct((CORES, *sums.shape[1:]), jnp.float32)
    own, other = pl.pallas_call(
        far_sum_kernel,
        in_specs=[VMEM] * (3 + len(operands)),
        out_specs=[VMEM, VMEM],
        out_shape=[sums, far_sums],
        scratch_shapes=[pltpu.VMEM((chip_count, chip_count), jnp.float32)],
        compiler_params=params(),
        cost_estimate=cost(flops, 4 * screened.size),
    )(screened, own, to_other_core(other), *operands)
    start = (far_block(), 0, 0, 0)
    far_own = lax.dynamic_slice(own, start, far_sums.shape) + to_other_core(other)
    return lax.dynamic_update_slice(own, far_own, start)


def shards(three_center, tile_mask, atom_order, green_occ, green_virt):
    p_count, row_count, width = three_center.shape
    ri_count, ao_count = lax.axis_size("ri"), lax.axis_size("ao")
    sig_count = width // ri_count // CORES
    chip_count = CORES * p_count

    def spread(block):
        return lax.all_to_all(block, "ri", split_axis=0, concat_axis=0, tiled=True)

    def to_other_core(block):
        return lax.ppermute(block, "ao", [(i, i ^ 1) for i in range(ao_count)])

    def along_x(block, shift):
        moves = [(i, (i + CORES * shift) % ao_count) for i in range(ao_count)]
        return lax.ppermute(block, "ao", moves)

    def along_x_all(block):
        return [block] + [along_x(block, shift) for shift in SHIFTS[1:]]

    def to_both_cores(blocks):
        own = jnp.stack(blocks)
        return own, to_other_core(own)

    def far_blocks(after, before, weight):
        half = jax.ShapeDtypeStruct((after.shape[0], width // 2, chip_count), jnp.bfloat16)
        low, high = pl.pallas_call(
            far_kernel,
            in_specs=[VMEM, VMEM],
            out_specs=[VMEM, VMEM],
            out_shape=[half, half],
            compiler_params=params(),
            cost_estimate=cost(weight, 4 * after.size),
        )(after, before)
        return [along_x(low, 1), along_x(high, -1)]

    other_center = to_other_core(three_center)
    rows_shape = jax.ShapeDtypeStruct((row_count, p_count, width), jnp.bfloat16)

    def screened_by_rows(own):
        return pl.pallas_call(
            lambda *refs: rows_kernel(own, *refs),
            in_specs=[HBM] * 3,
            out_specs=VMEM,
            out_shape=rows_shape,
            scratch_shapes=[
                pltpu.SMEM(atom_order.shape, jnp.int32),
                pltpu.VMEM(tile_mask.shape, jnp.int32),
                pltpu.VMEM(three_center.shape, jnp.bfloat16),
                pltpu.SemaphoreType.DMA((2 + p_count // 16,)),
            ],
            compiler_params=params(),
            cost_estimate=cost(10**9, 4 * three_center.size),
        )(in_hbm(atom_order), in_hbm(tile_mask), in_hbm(three_center) if own else other_center)

    virt, rows = lax.optimization_barrier(
        (along_x_all(green_virt), [screened_by_rows(True), screened_by_rows(False)])
    )
    greens_scratch = pltpu.VMEM((ao_count, *green_virt.shape), jnp.bfloat16)
    send_scratch = [
        pltpu.VMEM((row_count, width // CORES, chip_count), jnp.bfloat16),
        pltpu.VMEM((ri_count, sig_count, CORES, row_count, p_count), jnp.bfloat16),
        pltpu.SemaphoreType.DMA((ri_count // SEND_GROUP,)),
    ]
    send_shape = pltpu.HBM((ri_count, sig_count, CORES, row_count, p_count), jnp.bfloat16)
    kept_shape = pltpu.HBM(rows_shape.shape, jnp.bfloat16)
    send_half, *kept_rows = pl.pallas_call(
        half_kernel,
        in_specs=[VMEM] * 4,
        out_specs=[HBM] * 3,
        out_shape=[send_shape, kept_shape, kept_shape],
        scratch_shapes=[greens_scratch] + send_scratch + [pltpu.SemaphoreType.DMA((CORES,))],
        compiler_params=params(),
        cost_estimate=cost(2 * three_center.size * width, 6 * three_center.size),
    )(*rows, *to_both_cores(virt))
    half = spread(send_half)

    occ = pl.pallas_call(
        occ_kernel,
        in_specs=[pl.BlockSpec(memory_space=pltpu.SMEM), VMEM, VMEM],
        out_specs=VMEM,
        out_shape=jax.ShapeDtypeStruct((width, width), jnp.bfloat16),
        scratch_shapes=[greens_scratch],
        compiler_params=params(),
        cost_estimate=cost(4 * width**3, 8 * width * width),
    )(atom_order, *to_both_cores(along_x_all(green_occ)))
    send_screened = pl.pallas_call(
        screen_kernel,
        in_specs=[VMEM] * 2,
        out_specs=HBM,
        out_shape=send_shape,
        scratch_shapes=send_scratch,
        compiler_params=params(),
        cost_estimate=cost(0, 6 * three_center.size),
    )(*kept_rows)

    half, send_screened, occ = lax.optimization_barrier((half, send_screened, occ))
    screened = spread(send_screened)
    dressed_shape = jax.ShapeDtypeStruct((sig_count // PARTS, width, chip_count), jnp.bfloat16)
    dress_cost = cost(half.size * width, 3 * half.size)
    first_dressed, occ = pl.pallas_call(
        first_dress_kernel,
        in_specs=[VMEM, HBM],
        out_specs=[VMEM, VMEM],
        out_shape=[dressed_shape, jax.ShapeDtypeStruct(occ.shape, jnp.bfloat16)],
        scratch_shapes=[pltpu.SemaphoreType.DMA],
        compiler_params=params(),
        cost_estimate=dress_cost,
    )(half, in_hbm(occ))
    second_dressed = pl.pallas_call(
        lambda *refs: dress_sigs(sig_count // PARTS, *refs),
        in_specs=[VMEM, VMEM],
        out_specs=VMEM,
        out_shape=dressed_shape,
        compiler_params=params(),
        cost_estimate=dress_cost,
    )(half, occ)

    near, far = [], []
    for block, weight in ((first_dressed, 10**12), (second_dressed, 10**6)):
        after, before = along_x(block, 1), along_x(block, -1)
        near.append([block, after, before])
        far.append(far_blocks(after, before, weight))
    rows = ri_count // ao_count
    partial = product(screened, near, far, p_count, rows, to_other_core)
    return spread(partial.reshape(ri_count, p_count // rows, p_count)).sum(axis=0)


def solution(mesh):
    placed = (P("ao", "ri", None), P(), P(), P("ao", None), P("ao", None))
    return jax.shard_map(
        shards, mesh=mesh, in_specs=placed, out_specs=P("ri", "ao"), check_vma=False
    )
```
